256 devices in a mesh: patch: 64 (over y, x_lo, z), head: 4 (over x_hi, core).
Axes of the slice: x: 4 (x_hi: 2, x_lo: 2; x = x_hi * 2 + x_lo), y: 4, z: 8, core: 2. Of those that a mesh axis runs over, the one named last changes fastest.
Arguments:
- query: bfloat16 [12288, 2560], P('patch', 'head'), may hold values from -12 to 12
- key_fresh: bfloat16 [12288, 2560], P('patch', 'head'), may hold values from -6 to 6
- value_fresh: bfloat16 [12288, 2560], P('patch', 'head'), may hold values from -6 to 6
- key_stale: bfloat16 [12288, 2560], P('patch', 'head'), may hold values from -6 to 6
- value_stale: bfloat16 [12288, 2560], P('patch', 'head'), may hold values from -6 to 6
- out_weight: bfloat16 [2560, 5120], P('head'), may hold values from -0.125 to 0.125
- residual: bfloat16 [12288, 5120], P('patch', 'head'), may hold values from -6 to 6
- gate: bfloat16 [5120], P('head'), may hold values from 0.5 to 1.5
Outputs:
- updated: bfloat16 [12288, 5120], P('patch', 'head')
The draws below stay inside these ranges and needn't reach their ends.
All inputs are finite; a program needn't handle non-finite values.
Results may differ from the reference program's by a relative error of at most 0.0075.
Values may be sent and summed in bfloat16 or wider, within the bound.
No kernel may reach another device: no remote copies, remote signals or barrier semaphores. Data moves between devices by JAX's collectives and lax.ppermute only.
A program may use at most 128 MiB of HBM per device.

```python
import jax
import jax.numpy as jnp
from jax import lax

D = 5120
HD = 128
HEADS = 20
TOK_DEV = 192
TOKENS = 12288
N_PATCH = 64


def draw_query(key, part):
    key = jax.random.fold_in(key, 11)
    matrix = jnp.clip(jax.random.normal(key, (TOKENS, HEADS * HD), jnp.float32) * 3.0, -12.0, 12.0)
    return matrix.astype(jnp.bfloat16)


def draw_key_fresh(key, part):
    key = jax.random.fold_in(key, 23)
    matrix = jnp.clip(jax.random.normal(key, (TOKENS, HEADS * HD), jnp.float32), -6.0, 6.0)
    return matrix.astype(jnp.bfloat16)


def draw_key_stale(key, part):
    key = jax.random.fold_in(key, 37)
    matrix = jnp.clip(jax.random.normal(key, (TOKENS, HEADS * HD), jnp.float32), -6.0, 6.0)
    return matrix.astype(jnp.bfloat16)


def level_of(key, shape, pieces, least, top_value):
    level = 1.0
    for position, shards_of in pieces:
        heights = jax.random.uniform(jax.random.fold_in(jax.random.fold_in(key, 6), position), (shards_of,), jnp.float32, least / len(pieces), top_value / len(pieces))
        level = level * jnp.repeat(jnp.exp(heights), shape[position] // shards_of).reshape((-1,) + (1,) * (len(shape) - 1 - position))
    return level


def centred(own_key, extent, width, limit, cuts=(), kind=jnp.bfloat16):
    drawn = jax.random.normal(own_key, extent, jnp.float32) * width
    if len(cuts) > 0:
        drawn = level_of(own_key, extent, cuts, -0.22, 0.18) * drawn
    return jnp.clip(drawn, min=-limit, max=limit).astype(kind)


def setup_inputs(seed: int = 0) -> dict:
    seeds = jax.random.split(jax.random.key(seed), 9)
    return {
        "query": draw_query(jax.random.fold_in(seeds[8], 71), 0),
        "key_fresh": draw_key_fresh(jax.random.fold_in(seeds[8], 71), 0),
        "value_fresh": centred(seeds[2], (TOKENS, HEADS * HD), 1.0, 6.0, ((0, 64), (1, 4))),
        "key_stale": draw_key_stale(jax.random.fold_in(seeds[8], 71), 0),
        "value_stale": centred(seeds[4], (TOKENS, HEADS * HD), 1.0, 6.0, ((0, 64), (1, 4))),
        "out_weight": centred(seeds[5], (HEADS * HD, D), (HEADS * HD) ** -0.5, 0.125, ((0, 4),)),
        "residual": centred(seeds[6], (TOKENS, D), 1.0, 6.0, ((0, 64), (1, 4))),
        "gate": jnp.clip(0.5 + 1.0 * jax.random.uniform(seeds[7], (D,), jnp.float32) ** level_of(seeds[7], (D,), ((0, 4),), -0.2, 0.2), 0.5, 1.5).astype(jnp.bfloat16),
    }


def reference(query, key_fresh, value_fresh, key_stale, value_stale, out_weight, residual, gate):
    score_scale = HD ** -0.5
    gate_row = gate.astype(jnp.float32)

    def one_block(block_index):
        first_row = (block_index * TOK_DEV).astype(jnp.int32)
        query_rows = lax.dynamic_slice_in_dim(query, first_row, TOK_DEV, 0)
        fresh_keys = lax.dynamic_slice_in_dim(key_fresh, first_row, TOK_DEV, 0)
        fresh_values = lax.dynamic_slice_in_dim(value_fresh, first_row, TOK_DEV, 0)
        key_rows = lax.dynamic_update_slice_in_dim(key_stale, fresh_keys, first_row, 0)
        value_rows = lax.dynamic_update_slice_in_dim(value_stale, fresh_values, first_row, 0)
        queries = query_rows.astype(jnp.float32).reshape(TOK_DEV, HEADS, HD)
        key_cube = key_rows.astype(jnp.float32).reshape(TOKENS, HEADS, HD)
        value_cube = value_rows.astype(jnp.float32).reshape(TOKENS, HEADS, HD)
        scores = jnp.einsum("qhd,khd->hqk", queries, key_cube) * score_scale
        row_max = jnp.max(scores, axis=2, keepdims=True)
        weights = jnp.exp(scores - row_max)
        row_sum = jnp.sum(weights, axis=2)
        probabilities = lax.optimization_barrier(weights.astype(jnp.bfloat16)).astype(jnp.float32)
        mixture = jnp.einsum("hqk,khd->qhd", probabilities, value_cube)
        mixture = mixture / jnp.transpose(row_sum)[:, :, None]
        attended = mixture.astype(jnp.bfloat16).reshape(TOK_DEV, HEADS * HD)
        projected = jnp.dot(attended, out_weight, preferred_element_type=jnp.float32)
        skip_rows = lax.dynamic_slice_in_dim(residual, first_row, TOK_DEV, 0).astype(jnp.float32)
        return (skip_rows + gate_row[None, :] * projected).astype(jnp.bfloat16)

    blocks = lax.map(one_block, jnp.arange(N_PATCH, dtype=jnp.int32))
    return blocks.reshape(TOKENS, D)
```

```python
import functools
import math

import jax
import jax.numpy as jnp
from jax import lax
from jax.experimental import pallas as pl
from jax.experimental.pallas import tpu as pltpu
from jax.sharding import Mesh, PartitionSpec as P

HD = 128
EXP2_SCALE = HD ** (-0.5) * math.log2(math.e)
NY, NX, NZ = 4, 2, 8
GROUP = NY * NX
STAT_ROWS = 16


def attend_kernel(tiles, z_ref, *refs):
    query_refs = refs[:GROUP]
    k_ref, v_ref, fresh_k_ref, fresh_v_ref = refs[GROUP : GROUP + 4]
    out_refs = refs[GROUP + 4 : 2 * GROUP + 4]
    q_buf, k_buf, v_buf, o_buf, lse_buf = refs[2 * GROUP + 4 :]
    rows = query_refs[0].shape[0]
    key_rows = k_ref.shape[0]
    for slot in range(GROUP):
        q_buf[slot * rows : (slot + 1) * rows, :] = query_refs[(slot + 1) % GROUP][...]
    k_buf[...] = k_ref[...]
    v_buf[:, :HD] = v_ref[...]
    v_buf[:, HD:] = jnp.ones((key_rows, HD), jnp.bfloat16)

    def tile(first, count):
        scores = lax.dot_general(
            q_buf[first : first + count, :],
            k_buf[...],
            (((1,), (1,)), ((), ())),
            preferred_element_type=jnp.float32,
        )
        top = jnp.max(scores, axis=1, keepdims=True)
        weights = jnp.exp2((scores - top) * EXP2_SCALE).astype(jnp.bfloat16)
        mixed = jnp.dot(weights, v_buf[...], preferred_element_type=jnp.float32)
        row_sum = mixed[:, HD:]
        o_buf[first : first + count, :] = (mixed[:, :HD] / row_sum).astype(jnp.bfloat16)
        lse_buf[first : first + count, :] = top * EXP2_SCALE + jnp.log2(row_sum)

    first = 0
    for count in tiles:
        tile(first, count)
        first += count
    own = pl.ds(pl.multiple_of(z_ref[0] * rows, rows), rows)
    k_buf[own, :] = fresh_k_ref[...]
    v_buf[own, :HD] = fresh_v_ref[...]
    tile(first, rows)
    for slot in range(GROUP):
        out_ref = out_refs[(slot + 1) % GROUP]
        out_ref[:rows, :] = o_buf[slot * rows : (slot + 1) * rows, :]
        left = jnp.transpose(lse_buf[slot * rows : (slot + 1) * rows, :])[:1, :]
        stat = []
        for _ in range(3):
            part = left.astype(jnp.bfloat16).astype(jnp.float32)
            left = left - part
            stat += [part[:, :HD], jnp.concatenate([part[:, HD:], part[:, HD:]], axis=1)]
        stat.append(jnp.zeros((STAT_ROWS - 6, HD), jnp.float32))
        out_ref[rows:, :] = jnp.concatenate(stat, axis=0).astype(jnp.bfloat16)


def attend(z_index, queries, keys_values, fresh, heads):
    rows = queries[0].shape[0]
    key_rows = keys_values.shape[0]
    q_spec = pl.BlockSpec((rows, HD), lambda h: (0, h))
    return pl.pallas_call(
        functools.partial(attend_kernel, (448, 448, 448)),
        grid=(heads,),
        in_specs=[pl.BlockSpec(memory_space=pltpu.SMEM)]
        + [q_spec] * GROUP
        + [
            pl.BlockSpec((key_rows, HD), lambda h: (0, h)),
            pl.BlockSpec((key_rows, HD), lambda h: (0, h + heads)),
            pl.BlockSpec((rows, HD), lambda h: (0, h)),
            pl.BlockSpec((rows, HD), lambda h: (0, h + heads)),
        ],
        out_specs=[pl.BlockSpec((rows + STAT_ROWS, HD), lambda h: (0, h))] * GROUP,
        out_shape=[jax.ShapeDtypeStruct((rows + STAT_ROWS, heads * HD), jnp.bfloat16)] * GROUP,
        scratch_shapes=[
            pltpu.VMEM((GROUP * rows, HD), jnp.bfloat16),
            pltpu.VMEM((key_rows, HD), jnp.bfloat16),
            pltpu.VMEM((key_rows, 2 * HD), jnp.bfloat16),
            pltpu.VMEM((GROUP * rows, HD), jnp.bfloat16),
            pltpu.VMEM((GROUP * rows, HD), jnp.float32),
        ],
        compiler_params=pltpu.CompilerParams(vmem_limit_bytes=48 * 2**20),
        name="attend",
    )(z_index, *queries, keys_values, keys_values, fresh, fresh)


def combine_kernel(*refs):
    part_refs, out_ref = refs[:GROUP], refs[GROUP]
    rows, width = out_ref.shape
    heads = width // HD
    shares = []
    for head in range(heads):
        columns = slice(head * HD, (head + 1) * HD)
        lse = []
        for ref in part_refs:
            stat = ref[rows:, columns].astype(jnp.float32)
            first = stat[0:1] + stat[2:3] + stat[4:5]
            second = stat[1:2] + stat[3:4] + stat[5:6]
            lse.append(jnp.concatenate([first, second[:, : rows - HD]], axis=1))
        lse = jnp.concatenate(lse, axis=0)
        share = jnp.exp2(lse - jnp.max(lse, axis=0, keepdims=True))
        shares.append(share / jnp.sum(share, axis=0, keepdims=True))
    shares.append(jnp.zeros((HD - heads * GROUP, rows), jnp.float32))
    by_row = jnp.transpose(jnp.concatenate(shares, axis=0))
    for head in range(heads):
        columns = slice(head * HD, (head + 1) * HD)
        total = jnp.zeros((rows, HD), jnp.float32)
        for slot, ref in enumerate(part_refs):
            at = head * GROUP + slot
            total = total + by_row[:, at : at + 1] * ref[:rows, columns].astype(jnp.float32)
        out_ref[:, columns] = total.astype(jnp.bfloat16)


def combine(parts):
    rows, width = parts[0].shape
    return pl.pallas_call(
        combine_kernel,
        out_shape=jax.ShapeDtypeStruct((rows - STAT_ROWS, width), jnp.bfloat16),
        compiler_params=pltpu.CompilerParams(vmem_limit_bytes=32 * 2**20),
        name="combine",
    )(*parts)


def move_yx(array, dy, dx):
    pairs = [
        (y * NX + x, ((y + dy) % NY) * NX + (x + dx) % NX) for y in range(NY) for x in range(NX)
    ]
    return lax.ppermute(array, ("y", "x_lo"), pairs)


OFFSETS = [(dy, dx) for dy in range(NY) for dx in range(NX)]


def shards(query, key_fresh, value_fresh, key_stale, value_stale, out_weight, residual, gate):
    width = query.shape[1]
    heads = width // HD
    columns = residual.shape[1]
    x_hi, core = lax.axis_index("x_hi"), lax.axis_index("core")
    z_index = lax.axis_index("z").astype(jnp.int32).reshape(1)
    keys_values = lax.all_gather(
        jnp.concatenate([key_stale, value_stale], axis=1), "z", axis=0, tiled=True
    )
    fresh = jnp.concatenate([key_fresh, value_fresh], axis=1)
    queries = [query] + [move_yx(query, dy, dx) for dy, dx in OFFSETS[1:]]

    def weight_columns(x_half, core_half):
        return lax.dynamic_slice_in_dim(out_weight, (x_half * 2 + core_half) * columns, columns, 1)

    swap = [(0, 1), (1, 0)]
    sibling_weight = lax.ppermute(
        jnp.stack([weight_columns(1 - x_hi, 1 - core), weight_columns(x_hi, 1 - core)]),
        "core",
        swap,
    )
    own_weight = [weight_columns(1 - x_hi, core), weight_columns(x_hi, core)]

    partials = attend(z_index, queries, keys_values, fresh, heads)
    returned = [partials[0]] + [
        move_yx(part, -dy, -dx) for part, (dy, dx) in zip(partials[1:], OFFSETS[1:])
    ]
    attended = combine(returned)
    sibling = lax.ppermute(attended, "core", swap)

    def project(half):
        return jnp.dot(
            attended, own_weight[half], preferred_element_type=jnp.float32
        ) + jnp.dot(sibling, sibling_weight[half], preferred_element_type=jnp.float32)

    received = lax.ppermute(project(0).astype(jnp.bfloat16), "x_hi", swap)
    projected = project(1) + received.astype(jnp.float32)
    return (
        residual.astype(jnp.float32) + gate.astype(jnp.float32)[None, :] * projected
    ).astype(jnp.bfloat16)


def solution(mesh):
    axes = ("y", "x_lo", "z", "x_hi", "core")
    fine = Mesh(mesh.devices.reshape(NY, NX, NZ, 2, 2), axes)
    rows, cols = ("y", "x_lo", "z"), ("x_hi", "core")
    return jax.shard_map(
        shards,
        mesh=fine,
        in_specs=(
            P(rows, cols),
            P(rows, cols),
            P(rows, cols),
            P(rows, cols),
            P(rows, cols),
            P(cols, None),
            P(rows, cols),
            P(cols),
        ),
        out_specs=P(rows, cols),
        check_vma=False,
    )
```

```python
import functools
import math

import jax
import jax.numpy as jnp
from jax import lax
from jax.experimental import pallas as pl
from jax.experimental.pallas import tpu as pltpu
from jax.sharding import Mesh, PartitionSpec as P

HD = 128
EXP2_SCALE = HD ** (-0.5) * math.log2(math.e)
NY, NX, NZ = 4, 2, 8
STAT_ROWS = 16
BIG = 60
OFFSETS = [(dy, dx) for dy in range(NY) for dx in range(NX)]


def pipelined(tile_count, scores_of, finish):
    scores = scores_of(0)
    for index in range(tile_count):
        following = scores_of(index + 1) if index + 1 < tile_count else None
        finish(index, scores)
        scores = following


def multiply_keys(queries, keys):
    return lax.dot_general(
        queries, keys, (((1,), (1,)), ((), ())), preferred_element_type=jnp.float32
    )


def mix(scores, values):
    top = jnp.max(scores, axis=1, keepdims=True)
    weights = jnp.exp2((scores - top) * EXP2_SCALE).astype(jnp.bfloat16)
    mixed = jnp.dot(weights, values, preferred_element_type=jnp.float32)
    return top * EXP2_SCALE, mixed[:, :HD], mixed[:, HD:]


def attention_cost(products):
    return pl.CostEstimate(flops=16 * products, bytes_accessed=0, transcendentals=products // HD)


class Arrivals:
    def __init__(self, sems):
        self.sems, self.copies, self.open = sems, [], []

    def start(self, source, target):
        copy = pltpu.make_async_copy(source, target, self.sems.at[len(self.copies)])
        copy.start()
        self.copies.append(copy)
        self.open.append(True)
        return len(self.copies) - 1

    def wait(self, *names):
        for name in names:
            if self.open[name]:
                self.copies[name].wait()
                self.open[name] = False


def head_columns(head):
    return slice(head * HD, (head + 1) * HD)


def with_ones(values):
    return jnp.concatenate([values, jnp.ones(values.shape, values.dtype)], axis=1)


def stat_rows(column):
    lines = []
    for first in range(0, column.shape[0], HD):
        piece = column[first : first + HD, :]
        on_diagonal = lax.broadcasted_iota(jnp.int32, piece.shape, 0) == lax.broadcasted_iota(
            jnp.int32, piece.shape, 1
        )
        lines.append(jnp.sum(jnp.where(on_diagonal, piece, 0.0), axis=0, keepdims=True))
    left = jnp.concatenate(lines, axis=0)
    stat = []
    for _ in range(3):
        part = left.astype(jnp.bfloat16).astype(jnp.float32)
        left = left - part
        stat.append(part)
    stat.append(jnp.zeros((STAT_ROWS - 6, HD), jnp.float32))
    return jnp.concatenate(stat, axis=0).astype(jnp.bfloat16)


def attend_kernel(groups, blocks, place_ref, query_ref, around_ref, *refs):
    block_refs, refs = refs[:blocks], refs[blocks:]
    k_refs, v_refs = block_refs[::2], block_refs[1::2]
    fresh_k_ref, fresh_v_ref, out_ref, refs = *refs[:3], refs[3:]
    q_buf, k_buf, v_buf, fresh_k, fresh_v, out_buf, sems = refs
    rows, width = query_ref.shape
    heads = width // HD
    arrivals = Arrivals(sems)
    got_q = {}
    y, x = place_ref[0], place_ref[1]

    def lines(slot, count=1):
        return pl.ds(slot * rows, count * rows)

    def source(slot):
        dy, dx = OFFSETS[slot]
        return lax.rem(y + NY - dy, NY), lax.rem(x + NX - dx, NX)

    def fetch(group):
        first, count = group[0], len(group)
        if first:
            dx = OFFSETS[first][1]
            from_ref = around_ref.at[source(first)[0], pl.ds(dx * rows, count * rows)]
        else:
            from_ref = query_ref
        got_q[group] = arrivals.start(from_ref, q_buf.at[lines(first, count)])

    fetch(groups[0])
    got_k = [arrivals.start(ref, k_buf.at[lines(i)]) for i, ref in enumerate(k_refs)]
    got_v = [arrivals.start(ref, v_buf.at[lines(i)]) for i, ref in enumerate(v_refs)]
    for group in groups[1:]:
        fetch(group)
    got_fresh_k = arrivals.start(fresh_k_ref, fresh_k)
    got_fresh_v = arrivals.start(fresh_v_ref, fresh_v)
    tiles = [(group, head) for group in groups for head in range(heads)]

    def scores_of(i):
        group, head = tiles[i]
        columns = head_columns(head)
        arrivals.wait(got_q[group], *got_k)
        keys = k_buf[:, columns]
        if 0 in group:
            arrivals.wait(got_fresh_k)
            keys = jnp.concatenate([fresh_k[:, columns], k_buf[rows:, columns]], axis=0)
        return multiply_keys(q_buf[lines(group[0], len(group)), columns], keys)

    def finish(i, scores):
        group, head = tiles[i]
        columns = head_columns(head)
        arrivals.wait(*got_v)
        values = v_buf[:, columns]
        if 0 in group:
            arrivals.wait(got_fresh_v)
            values = jnp.concatenate([fresh_v[:, columns], v_buf[rows:, columns]], axis=0)
        top, mixed, row_sum = mix(scores, with_ones(values))
        mixture = (mixed / row_sum).astype(jnp.bfloat16)
        lse = top + jnp.log2(row_sum)
        for i, slot in enumerate(group):
            at = slice(i * rows, (i + 1) * rows)
            out_buf[slot, :rows, columns] = mixture[at]
            out_buf[slot, rows:, columns] = stat_rows(lse[at])
            if head == heads - 1:
                to_y, to_x = source(slot)
                arrivals.start(out_buf.at[slot], out_ref.at[to_y * NX + to_x])

    pipelined(len(tiles), scores_of, finish)
    arrivals.wait(*range(len(arrivals.copies)))


def attend(groups, place, query, around, blocks, fresh_key, fresh_value):
    rows, width = query.shape
    slots, count = len(OFFSETS), len(blocks)
    anywhere = pl.BlockSpec(memory_space=pl.ANY)
    return pl.pallas_call(
        functools.partial(attend_kernel, groups, 2 * count),
        in_specs=[pl.BlockSpec(memory_space=pltpu.SMEM)] + [anywhere] * (4 + 2 * count),
        out_specs=anywhere,
        out_shape=jax.ShapeDtypeStruct((slots, rows + STAT_ROWS, width), jnp.bfloat16),
        scratch_shapes=[
            pltpu.VMEM((slots * rows, width), jnp.bfloat16),
            pltpu.VMEM((count * rows, width), jnp.bfloat16),
            pltpu.VMEM((count * rows, width), jnp.bfloat16),
            pltpu.VMEM((rows, width), jnp.bfloat16),
            pltpu.VMEM((rows, width), jnp.bfloat16),
            pltpu.VMEM((slots, rows + STAT_ROWS, width), jnp.bfloat16),
            pltpu.SemaphoreType.DMA((2 * slots + 2 * count + 2,)),
        ],
        compiler_params=pltpu.CompilerParams(vmem_limit_bytes=BIG * 2**20),
        cost_estimate=attention_cost(slots * rows * count * rows * width),
        name="attend",
    )(
        place,
        query,
        around,
        *[array for block in blocks for array in block],
        fresh_key,
        fresh_value,
    )


def repeat_kernel(a_ref, b_ref, out_ref):
    rows = a_ref.shape[0]
    out_ref[:rows, :] = a_ref[...]
    out_ref[rows:, :] = b_ref[...]


def repeat(a, b, times):
    rows, width = a.shape
    whole = pl.BlockSpec((rows, width), lambda i: (0, 0))
    return pl.pallas_call(
        repeat_kernel,
        grid=(times,),
        in_specs=[whole, whole],
        out_specs=pl.BlockSpec((None, 2 * rows, width), lambda i: (i, 0, 0)),
        out_shape=jax.ShapeDtypeStruct((times, 2 * rows, width), a.dtype),
        compiler_params=pltpu.CompilerParams(vmem_limit_bytes=BIG * 2**20),
        name="repeat",
    )(a, b)


def combine_kernel(blocks_ref, parts_ref, w_ref, out_ref, first_ref, second_ref, w_buf, sems):
    product_refs = (first_ref, second_ref)
    columns = first_ref.shape[1]
    copies = []
    for i in range(len(product_refs)):
        first = pl.multiple_of(blocks_ref[i] * columns, columns)
        copy = pltpu.make_async_copy(w_ref.at[:, pl.ds(first, columns)], w_buf.at[i], sems.at[i])
        copy.start()
        copies.append(copy)
    group = parts_ref.shape[0]
    rows, width = out_ref.shape
    heads = width // HD
    shares = []
    for head in range(heads):
        columns = slice(head * HD, (head + 1) * HD)
        lse = []
        for part in range(group):
            stat = parts_ref[part, rows:, columns].astype(jnp.float32)
            lines = stat[0:2] + stat[2:4] + stat[4:6]
            lse.append(jnp.concatenate([lines[:1], lines[1:2, : rows - HD]], axis=1))
        lse = jnp.concatenate(lse, axis=0)
        share = jnp.exp2(lse - jnp.max(lse, axis=0, keepdims=True))
        shares.append(share / jnp.sum(share, axis=0, keepdims=True))
    shares.append(jnp.zeros((HD - heads * group, rows), jnp.float32))
    by_row = jnp.transpose(jnp.concatenate(shares, axis=0))
    for head in range(heads):
        columns = slice(head * HD, (head + 1) * HD)
        total = jnp.zeros((rows, HD), jnp.float32)
        for part in range(group):
            at = head * group + part
            mixture = parts_ref[part, :rows, columns].astype(jnp.float32)
            total = total + by_row[:, at : at + 1] * mixture
        out_ref[:, columns] = total.astype(jnp.bfloat16)
    for i, product_ref in enumerate(product_refs):
        copies[i].wait()
        product_ref[...] = jnp.dot(
            out_ref[...], w_buf[i], preferred_element_type=jnp.float32
        ).astype(jnp.bfloat16)


def combine(blocks, parts, out_weight, columns):
    _, rows, width = parts.shape
    rows -= STAT_ROWS
    vmem = pl.BlockSpec(memory_space=pltpu.VMEM)
    return pl.pallas_call(
        combine_kernel,
        in_specs=[
            pl.BlockSpec(memory_space=pltpu.SMEM),
            vmem,
            pl.BlockSpec(memory_space=pl.ANY),
        ],
        out_specs=[vmem, vmem, vmem],
        out_shape=[
            jax.ShapeDtypeStruct((rows, width), jnp.bfloat16),
            jax.ShapeDtypeStruct((rows, columns), jnp.bfloat16),
            jax.ShapeDtypeStruct((rows, columns), jnp.bfloat16),
        ],
        scratch_shapes=[
            pltpu.VMEM((2, width, columns), jnp.bfloat16),
            pltpu.SemaphoreType.DMA((2,)),
        ],
        compiler_params=pltpu.CompilerParams(vmem_limit_bytes=BIG * 2**20),
        name="combine",
    )(blocks, parts, out_weight)


def project_kernel(block_ref, a_ref, w_ref, out_ref):
    out_ref[...] = jnp.dot(
        a_ref[...], w_ref[...], preferred_element_type=jnp.float32
    ).astype(out_ref.dtype)


def project(block, attended, out_weight, columns, dtype):
    rows, width = attended.shape
    steps = 2
    part = columns // steps
    return pl.pallas_call(
        project_kernel,
        grid_spec=pltpu.PrefetchScalarGridSpec(
            num_scalar_prefetch=1,
            grid=(steps,),
            in_specs=[
                pl.BlockSpec((rows, width), lambda i, block: (0, 0)),
                pl.BlockSpec((width, part), lambda i, block: (0, block[0] * steps + i)),
            ],
            out_specs=pl.BlockSpec((rows, part), lambda i, block: (0, i)),
        ),
        out_shape=jax.ShapeDtypeStruct((rows, columns), dtype),
        compiler_params=pltpu.CompilerParams(vmem_limit_bytes=BIG * 2**20),
        name="project",
    )(block, attended, out_weight)


def move_z(array, step):
    return lax.ppermute(array, "z", [(z, (z + step) % NZ) for z in range(NZ)])


def shards(query, key_fresh, value_fresh, key_stale, value_stale, out_weight, residual, gate):
    columns = residual.shape[1]
    x_hi, core = lax.axis_index("x_hi"), lax.axis_index("core")

    swap = [(0, 1), (1, 0)]
    stacked = repeat(query, lax.ppermute(query, "x_lo", swap), NY)
    own = (key_stale, value_stale)
    up, down = [own], [own]
    for step in range(1, NZ // 2):
        up.append(tuple(move_z(array, 1) for array in up[-1]))
        down.append(tuple(move_z(array, -1) for array in down[-1]))
        if step == 1:
            up[1], down[1], stacked = lax.optimization_barrier((up[1], down[1], stacked))
            around = lax.all_to_all(stacked, "y", 0, 0)
    far = (move_z(up[-1][0], 1), move_z(down[-1][1], -1))
    partials = attend(
        ((2, 3), (4, 5), (6, 7), (1,), (0,)),
        jnp.stack([lax.axis_index("y"), lax.axis_index("x_lo")]).astype(jnp.int32),
        query,
        around,
        up + down[1:] + [far],
        key_fresh,
        value_fresh,
    )
    returned = lax.all_to_all(partials, ("y", "x_lo"), 0, 0)

    def block(x_half, core_half):
        return (x_half * 2 + core_half).astype(jnp.int32).reshape(1)

    attended, for_core, for_core_late = combine(
        jnp.concatenate([block(1 - x_hi, 1 - core), block(x_hi, 1 - core)]),
        returned,
        out_weight,
        columns,
    )
    from_core = lax.ppermute(for_core, "core", swap).astype(jnp.float32)
    chip_sum = project(block(1 - x_hi, core), attended, out_weight, columns, jnp.float32)
    chip_sum = (chip_sum + from_core).astype(jnp.bfloat16)
    from_x = lax.ppermute(chip_sum, "x_hi", swap)
    attended, for_core_late, _ = lax.optimization_barrier((attended, for_core_late, chip_sum))
    from_core = lax.ppermute(for_core_late, "core", swap)
    total = project(block(x_hi, core), attended, out_weight, columns, jnp.float32)
    total = total + from_core.astype(jnp.float32)
    total = total + from_x.astype(jnp.float32)
    return (
        residual.astype(jnp.float32) + gate.astype(jnp.float32)[None, :] * total
    ).astype(jnp.bfloat16)


def solution(mesh):
    axes = ("y", "x_lo", "z", "x_hi", "core")
    fine = Mesh(mesh.devices.reshape(NY, NX, NZ, 2, 2), axes)
    rows, cols = ("y", "x_lo", "z"), ("x_hi", "core")
    return jax.shard_map(
        shards,
        mesh=fine,
        in_specs=(
            P(rows, cols),
            P(rows, cols),
            P(rows, cols),
            P(rows, cols),
            P(rows, cols),
            P(cols, None),
            P(rows, cols),
            P(cols),
        ),
        out_specs=P(rows, cols),
        check_vma=False,
    )
```

```python
import functools
import math

import jax
import jax.numpy as jnp
from jax import lax
from jax.experimental import pallas as pl
from jax.experimental.pallas import tpu as pltpu
from jax.sharding import Mesh, PartitionSpec as P

HD = 128
EXP2_SCALE = HD ** (-0.5) * math.log2(math.e)
NY, NX, NZ = 4, 2, 8
STAT_ROWS = 16
BIG = 60
OFFSETS = [(dy, dx) for dy in range(NY) for dx in range(NX)]


def pipelined(tile_count, scores_of, finish):
    scores = scores_of(0)
    for index in range(tile_count):
        following = scores_of(index + 1) if index + 1 < tile_count else None
        finish(index, scores)
        scores = following


def multiply_keys(queries, keys):
    return lax.dot_general(
        queries, keys, (((1,), (1,)), ((), ())), preferred_element_type=jnp.float32
    )


def mix(scores, values):
    top = jnp.max(scores, axis=1, keepdims=True)
    weights = jnp.exp2((scores - top) * EXP2_SCALE).astype(jnp.bfloat16)
    mixed = jnp.dot(weights, values, preferred_element_type=jnp.float32)
    return top * EXP2_SCALE, mixed[:, :HD], mixed[:, HD:]


def attention_cost(products):
    return pl.CostEstimate(flops=16 * products, bytes_accessed=0, transcendentals=products // HD)


class Arrivals:
    def __init__(self, sems):
        self.sems, self.copies, self.open = sems, [], []

    def start(self, source, target):
        copy = pltpu.make_async_copy(source, target, self.sems.at[len(self.copies)])
        copy.start()
        self.copies.append(copy)
        self.open.append(True)
        return len(self.copies) - 1

    def wait(self, *names):
        for name in names:
            if self.open[name]:
                self.copies[name].wait()
                self.open[name] = False


def head_columns(head):
    return slice(head * HD, (head + 1) * HD)


def with_ones(values):
    return jnp.concatenate([values, jnp.ones(values.shape, values.dtype)], axis=1)


def stat_rows(column):
    lines = []
    for first in range(0, column.shape[0], HD):
        piece = column[first : first + HD, :]
        on_diagonal = lax.broadcasted_iota(jnp.int32, piece.shape, 0) == lax.broadcasted_iota(
            jnp.int32, piece.shape, 1
        )
        lines.append(jnp.sum(jnp.where(on_diagonal, piece, 0.0), axis=0, keepdims=True))
    left = jnp.concatenate(lines, axis=0)
    stat = []
    for _ in range(3):
        part = left.astype(jnp.bfloat16).astype(jnp.float32)
        left = left - part
        stat.append(part)
    stat.append(jnp.zeros((STAT_ROWS - 6, HD), jnp.float32))
    return jnp.concatenate(stat, axis=0).astype(jnp.bfloat16)


def attend_kernel(groups, blocks, first_head, place_ref, query_ref, around_ref, *refs):
    block_refs, refs = refs[:blocks], refs[blocks:]
    k_refs, v_refs = block_refs[::2], block_refs[1::2]
    fresh_k_ref, fresh_v_ref, out_ref, refs = *refs[:3], refs[3:]
    q_buf, k_buf, v_buf, fresh_k, fresh_v, out_buf, sems = refs
    rows, width = fresh_k.shape
    heads = width // HD
    taken = pl.ds(first_head * HD, width)
    arrivals = Arrivals(sems)
    got_q = {}
    y, x = place_ref[0], place_ref[1]

    def lines(slot, count=1):
        return pl.ds(slot * rows, count * rows)

    def source(slot):
        dy, dx = OFFSETS[slot]
        return lax.rem(y + NY - dy, NY), lax.rem(x + NX - dx, NX)

    def fetch(group):
        first, count = group[0], len(group)
        if first:
            dx = OFFSETS[first][1]
            from_ref = around_ref.at[source(first)[0], pl.ds(dx * rows, count * rows), taken]
        else:
            from_ref = query_ref.at[:, taken]
        got_q[group] = arrivals.start(from_ref, q_buf.at[lines(first, count)])

    fetch(groups[0])
    got_k = [arrivals.start(ref.at[:, taken], k_buf.at[lines(i)]) for i, ref in enumerate(k_refs)]
    got_v = [arrivals.start(ref.at[:, taken], v_buf.at[lines(i)]) for i, ref in enumerate(v_refs)]
    for group in groups[1:]:
        fetch(group)
    got_fresh_k = arrivals.start(fresh_k_ref.at[:, taken], fresh_k)
    got_fresh_v = arrivals.start(fresh_v_ref.at[:, taken], fresh_v)
    tiles = [(group, head) for group in groups for head in range(heads)]

    def scores_of(i):
        group, head = tiles[i]
        columns = head_columns(head)
        arrivals.wait(got_q[group], *got_k)
        keys = k_buf[:, columns]
        if 0 in group:
            arrivals.wait(got_fresh_k)
            keys = jnp.concatenate([fresh_k[:, columns], k_buf[rows:, columns]], axis=0)
        return multiply_keys(q_buf[lines(group[0], len(group)), columns], keys)

    def finish(i, scores):
        group, head = tiles[i]
        columns = head_columns(head)
        arrivals.wait(*got_v)
        values = v_buf[:, columns]
        if 0 in group:
            arrivals.wait(got_fresh_v)
            values = jnp.concatenate([fresh_v[:, columns], v_buf[rows:, columns]], axis=0)
        top, mixed, row_sum = mix(scores, with_ones(values))
        mixture = (mixed / row_sum).astype(jnp.bfloat16)
        lse = top + jnp.log2(row_sum)
        for i, slot in enumerate(group):
            at = slice(i * rows, (i + 1) * rows)
            out_buf[slot, :rows, columns] = mixture[at]
            out_buf[slot, rows:, columns] = stat_rows(lse[at])
            if head == heads - 1:
                to_y, to_x = source(slot)
                arrivals.start(out_buf.at[slot], out_ref.at[to_y * NX + to_x])

    pipelined(len(tiles), scores_of, finish)
    arrivals.wait(*range(len(arrivals.copies)))


def attend(groups, heads, place, query, around, blocks, fresh_key, fresh_value):
    rows, width = query.shape[0], len(heads) * HD
    slots, count = len(OFFSETS), len(blocks)
    anywhere = pl.BlockSpec(memory_space=pl.ANY)
    return pl.pallas_call(
        functools.partial(attend_kernel, groups, 2 * count, heads[0]),
        in_specs=[pl.BlockSpec(memory_space=pltpu.SMEM)] + [anywhere] * (4 + 2 * count),
        out_specs=anywhere,
        out_shape=jax.ShapeDtypeStruct((slots, rows + STAT_ROWS, width), jnp.bfloat16),
        scratch_shapes=[
            pltpu.VMEM((slots * rows, width), jnp.bfloat16),
            pltpu.VMEM((count * rows, width), jnp.bfloat16),
            pltpu.VMEM((count * rows, width), jnp.bfloat16),
            pltpu.VMEM((rows, width), jnp.bfloat16),
            pltpu.VMEM((rows, width), jnp.bfloat16),
            pltpu.VMEM((slots, rows + STAT_ROWS, width), jnp.bfloat16),
            pltpu.SemaphoreType.DMA((2 * slots + 2 * count + 2,)),
        ],
        compiler_params=pltpu.CompilerParams(vmem_limit_bytes=BIG * 2**20),
        cost_estimate=attention_cost(slots * rows * count * rows * width),
        name="attend",
    )(
        place,
        query,
        around,
        *[array for block in blocks for array in block],
        fresh_key,
        fresh_value,
    )


def last_kernel(place_ref, keys_ref, values_ref, out_ref):
    for i in range(out_ref.shape[0]):
        out_ref[i] = place_ref[i]


def last_of(place, keys, values):
    smem, anywhere = pl.BlockSpec(memory_space=pltpu.SMEM), pl.BlockSpec(memory_space=pl.ANY)
    return pl.pallas_call(
        last_kernel,
        in_specs=[smem, anywhere, anywhere],
        out_specs=smem,
        out_shape=jax.ShapeDtypeStruct(place.shape, place.dtype),
        cost_estimate=pl.CostEstimate(flops=13 * 10**9, bytes_accessed=0, transcendentals=0),
        name="last_of",
    )(place, keys, values)


def repeat_kernel(a_ref, b_ref, out_ref):
    rows = a_ref.shape[0]
    out_ref[:rows, :] = a_ref[...]
    out_ref[rows:, :] = b_ref[...]


def repeat(a, b, times):
    rows, width = a.shape
    whole = pl.BlockSpec((rows, width), lambda i: (0, 0))
    return pl.pallas_call(
        repeat_kernel,
        grid=(times,),
        in_specs=[whole, whole],
        out_specs=pl.BlockSpec((None, 2 * rows, width), lambda i: (i, 0, 0)),
        out_shape=jax.ShapeDtypeStruct((times, 2 * rows, width), a.dtype),
        compiler_params=pltpu.CompilerParams(vmem_limit_bytes=BIG * 2**20),
        name="repeat",
    )(a, b)


def combine_kernel(blocks_ref, w_ref, *refs):
    *parts_refs, out_ref, first_ref, second_ref, w_buf, sems = refs
    product_refs = (first_ref, second_ref)
    columns = first_ref.shape[1]
    copies = []
    for i in range(len(product_refs)):
        first = pl.multiple_of(blocks_ref[i] * columns, columns)
        copy = pltpu.make_async_copy(w_ref.at[:, pl.ds(first, columns)], w_buf.at[i], sems.at[i])
        copy.start()
        copies.append(copy)
    group = parts_refs[0].shape[0]
    rows, width = out_ref.shape
    heads = width // HD
    where = [(ref, head_columns(i)) for ref in parts_refs for i in range(ref.shape[2] // HD)]
    shares = []
    for parts_ref, columns in where:
        lse = []
        for part in range(group):
            stat = parts_ref[part, rows:, columns].astype(jnp.float32)
            lines = stat[0:2] + stat[2:4] + stat[4:6]
            lse.append(jnp.concatenate([lines[:1], lines[1:2, : rows - HD]], axis=1))
        lse = jnp.concatenate(lse, axis=0)
        share = jnp.exp2(lse - jnp.max(lse, axis=0, keepdims=True))
        shares.append(share / jnp.sum(share, axis=0, keepdims=True))
    shares.append(jnp.zeros((HD - heads * group, rows), jnp.float32))
    by_row = jnp.transpose(jnp.concatenate(shares, axis=0))
    for head, (parts_ref, columns) in enumerate(where):
        total = jnp.zeros((rows, HD), jnp.float32)
        for part in range(group):
            at = head * group + part
            mixture = parts_ref[part, :rows, columns].astype(jnp.float32)
            total = total + by_row[:, at : at + 1] * mixture
        out_ref[:, head_columns(head)] = total.astype(jnp.bfloat16)
    for i, product_ref in enumerate(product_refs):
        copies[i].wait()
        product_ref[...] = jnp.dot(
            out_ref[...], w_buf[i], preferred_element_type=jnp.float32
        ).astype(jnp.bfloat16)


def combine(blocks, parts, out_weight, columns):
    rows = parts[0].shape[1] - STAT_ROWS
    width = sum(part.shape[2] for part in parts)
    vmem = pl.BlockSpec(memory_space=pltpu.VMEM)
    return pl.pallas_call(
        combine_kernel,
        in_specs=[
            pl.BlockSpec(memory_space=pltpu.SMEM),
            pl.BlockSpec(memory_space=pl.ANY),
            *[vmem] * len(parts),
        ],
        out_specs=[vmem, vmem, vmem],
        out_shape=[
            jax.ShapeDtypeStruct((rows, width), jnp.bfloat16),
            jax.ShapeDtypeStruct((rows, columns), jnp.bfloat16),
            jax.ShapeDtypeStruct((rows, columns), jnp.bfloat16),
        ],
        scratch_shapes=[
            pltpu.VMEM((2, width, columns), jnp.bfloat16),
            pltpu.SemaphoreType.DMA((2,)),
        ],
        compiler_params=pltpu.CompilerParams(vmem_limit_bytes=BIG * 2**20),
        name="combine",
    )(blocks, out_weight, *parts)


def project_kernel(block_ref, a_ref, w_ref, out_ref):
    out_ref[...] = jnp.dot(
        a_ref[...], w_ref[...], preferred_element_type=jnp.float32
    ).astype(out_ref.dtype)


def project(block, attended, out_weight, columns, dtype):
    rows, width = attended.shape
    steps = 2
    part = columns // steps
    return pl.pallas_call(
        project_kernel,
        grid_spec=pltpu.PrefetchScalarGridSpec(
            num_scalar_prefetch=1,
            grid=(steps,),
            in_specs=[
                pl.BlockSpec((rows, width), lambda i, block: (0, 0)),
                pl.BlockSpec((width, part), lambda i, block: (0, block[0] * steps + i)),
            ],
            out_specs=pl.BlockSpec((rows, part), lambda i, block: (0, i)),
        ),
        out_shape=jax.ShapeDtypeStruct((rows, columns), dtype),
        compiler_params=pltpu.CompilerParams(vmem_limit_bytes=BIG * 2**20),
        name="project",
    )(block, attended, out_weight)


def move_z(array, step):
    return lax.ppermute(array, "z", [(z, (z + step) % NZ) for z in range(NZ)])


def shards(query, key_fresh, value_fresh, key_stale, value_stale, out_weight, residual, gate):
    columns = residual.shape[1]
    x_hi, core = lax.axis_index("x_hi"), lax.axis_index("core")

    swap = [(0, 1), (1, 0)]
    stacked = repeat(query, lax.ppermute(query, "x_lo", swap), NY)
    own = (key_stale, value_stale)
    up, down = [own], [own]
    for step in range(1, NZ // 2):
        up.append(tuple(move_z(array, 1) for array in up[-1]))
        down.append(tuple(move_z(array, -1) for array in down[-1]))
    stacked = lax.optimization_barrier((stacked, up[1][0], down[1][0]))[0]
    around = lax.all_to_all(stacked, "y", 0, 0)
    far = (move_z(up[-1][0], 1), move_z(down[-1][1], -1))
    place = jnp.stack([lax.axis_index("y"), lax.axis_index("x_lo")]).astype(jnp.int32)
    place = last_of(place, *far)
    heads = query.shape[1] // HD
    partials = attend(
        ((2, 3), (4, 5), (6, 7), (1,), (0,)),
        range(heads),
        place,
        query,
        around,
        up + down[1:] + [far],
        key_fresh,
        value_fresh,
    )
    returned = [lax.all_to_all(partials, ("y", "x_lo"), 0, 0)]

    def block(x_half, core_half):
        return (x_half * 2 + core_half).astype(jnp.int32).reshape(1)

    attended, for_core, for_core_late = combine(
        jnp.concatenate([block(1 - x_hi, 1 - core), block(x_hi, 1 - core)]),
        returned,
        out_weight,
        columns,
    )
    from_core = lax.ppermute(for_core, "core", swap).astype(jnp.float32)
    chip_sum = project(block(1 - x_hi, core), attended, out_weight, columns, jnp.float32)
    chip_sum = (chip_sum + from_core).astype(jnp.bfloat16)
    from_x = lax.ppermute(chip_sum, "x_hi", swap)
    attended, for_core_late, _ = lax.optimization_barrier((attended, for_core_late, chip_sum))
    from_core = lax.ppermute(for_core_late, "core", swap)
    total = project(block(x_hi, core), attended, out_weight, columns, jnp.float32)
    gate_row = gate.astype(jnp.float32)[None, :]
    total = total + from_core.astype(jnp.float32)
    ready = lax.optimization_barrier(residual.astype(jnp.float32) + gate_row * total)
    return (ready + gate_row * from_x.astype(jnp.float32)).astype(jnp.bfloat16)


def solution(mesh):
    axes = ("y", "x_lo", "z", "x_hi", "core")
    fine = Mesh(mesh.devices.reshape(NY, NX, NZ, 2, 2), axes)
    rows, cols = ("y", "x_lo", "z"), ("x_hi", "core")
    return jax.shard_map(
        shards,
        mesh=fine,
        in_specs=(
            P(rows, cols),
            P(rows, cols),
            P(rows, cols),
            P(rows, cols),
            P(rows, cols),
            P(cols, None),
            P(rows, cols),
            P(cols),
        ),
        out_specs=P(rows, cols),
        check_vma=False,
    )
```

```python
import functools
import math

import jax
import jax.numpy as jnp
from jax import lax
from jax.experimental import pallas as pl
from jax.experimental.pallas import tpu as pltpu
from jax.sharding import Mesh, PartitionSpec as P

HD = 128
EXP2_SCALE = HD ** (-0.5) * math.log2(math.e)
NY, NX, NZ = 4, 2, 8
STAT_ROWS = 16
BIG, SMALL = 60, 16
OFFSETS = [(dy, dx) for dy in range(NY) for dx in range(NX)]


def pipelined(tile_count, scores_of, finish):
    scores = scores_of(0)
    for index in range(tile_count):
        following = scores_of(index + 1) if index + 1 < tile_count else None
        finish(index, scores)
        scores = following


def multiply_keys(queries, keys):
    return lax.dot_general(
        queries, keys, (((1,), (1,)), ((), ())), preferred_element_type=jnp.float32
    )


def mix(scores, values):
    top = jnp.max(scores, axis=1, keepdims=True)
    weights = jnp.exp2((scores - top) * EXP2_SCALE).astype(jnp.bfloat16)
    mixed = jnp.dot(weights, values, preferred_element_type=jnp.float32)
    return top * EXP2_SCALE, mixed[:, :HD], mixed[:, HD:]


def attention_cost(products):
    return pl.CostEstimate(flops=16 * products, bytes_accessed=0, transcendentals=products // HD)


class Arrivals:
    def __init__(self, sems):
        self.sems, self.copies, self.open = sems, [], []

    def start(self, source, target):
        copy = pltpu.make_async_copy(source, target, self.sems.at[len(self.copies)])
        copy.start()
        self.copies.append(copy)
        self.open.append(True)
        return len(self.copies) - 1

    def wait(self, *names):
        for name in names:
            if self.open[name]:
                self.copies[name].wait()
                self.open[name] = False


def head_columns(head):
    return slice(head * HD, (head + 1) * HD)


def with_ones(values):
    return jnp.concatenate([values, jnp.ones(values.shape, values.dtype)], axis=1)


def stat_rows(column):
    lines = []
    for first in range(0, column.shape[0], HD):
        piece = column[first : first + HD, :]
        on_diagonal = lax.broadcasted_iota(jnp.int32, piece.shape, 0) == lax.broadcasted_iota(
            jnp.int32, piece.shape, 1
        )
        lines.append(jnp.sum(jnp.where(on_diagonal, piece, 0.0), axis=0, keepdims=True))
    left = jnp.concatenate(lines, axis=0)
    stat = []
    for _ in range(3):
        part = left.astype(jnp.bfloat16).astype(jnp.float32)
        left = left - part
        stat.append(part)
    stat.append(jnp.zeros((STAT_ROWS - 6, HD), jnp.float32))
    return jnp.concatenate(stat, axis=0).astype(jnp.bfloat16)


def attend_kernel(groups, blocks, first_head, place_ref, query_ref, around_ref, *refs):
    block_refs, refs = refs[:blocks], refs[blocks:]
    k_refs, v_refs = block_refs[::2], block_refs[1::2]
    fresh_k_ref, fresh_v_ref, out_ref, refs = *refs[:3], refs[3:]
    q_buf, k_buf, v_buf, fresh_k, fresh_v, out_buf, sems = refs
    rows, width = fresh_k.shape
    heads = width // HD
    taken = pl.ds(first_head * HD, width)
    arrivals = Arrivals(sems)
    got_q = {}
    y, x = place_ref[0], place_ref[1]

    def lines(slot, count=1):
        return pl.ds(slot * rows, count * rows)

    def source(slot):
        dy, dx = OFFSETS[slot]
        return lax.rem(y + NY - dy, NY), lax.rem(x + NX - dx, NX)

    def fetch(group):
        first, count = group[0], len(group)
        if first:
            dx = OFFSETS[first][1]
            from_ref = around_ref.at[source(first)[0], pl.ds(dx * rows, count * rows), taken]
        else:
            from_ref = query_ref.at[:, taken]
        got_q[group] = arrivals.start(from_ref, q_buf.at[lines(first, count)])

    fetch(groups[0])
    got_k = [arrivals.start(ref.at[:, taken], k_buf.at[lines(i)]) for i, ref in enumerate(k_refs)]
    got_v = [arrivals.start(ref.at[:, taken], v_buf.at[lines(i)]) for i, ref in enumerate(v_refs)]
    for group in groups[1:]:
        fetch(group)
    got_fresh_k = arrivals.start(fresh_k_ref.at[:, taken], fresh_k)
    got_fresh_v = arrivals.start(fresh_v_ref.at[:, taken], fresh_v)
    tiles = [(group, head) for group in groups for head in range(heads)]

    def scores_of(i):
        group, head = tiles[i]
        columns = head_columns(head)
        arrivals.wait(got_q[group], *got_k)
        keys = k_buf[:, columns]
        if 0 in group:
            arrivals.wait(got_fresh_k)
            keys = jnp.concatenate([fresh_k[:, columns], k_buf[rows:, columns]], axis=0)
        return multiply_keys(q_buf[lines(group[0], len(group)), columns], keys)

    def finish(i, scores):
        group, head = tiles[i]
        columns = head_columns(head)
        arrivals.wait(*got_v)
        values = v_buf[:, columns]
        if 0 in group:
            arrivals.wait(got_fresh_v)
            values = jnp.concatenate([fresh_v[:, columns], v_buf[rows:, columns]], axis=0)
        top, mixed, row_sum = mix(scores, with_ones(values))
        mixture = (mixed / row_sum).astype(jnp.bfloat16)
        lse = top + jnp.log2(row_sum)
        for i, slot in enumerate(group):
            at = slice(i * rows, (i + 1) * rows)
            out_buf[slot, :rows, columns] = mixture[at]
            out_buf[slot, rows:, columns] = stat_rows(lse[at])
            if head == heads - 1:
                to_y, to_x = source(slot)
                arrivals.start(out_buf.at[slot], out_ref.at[to_y * NX + to_x])

    pipelined(len(tiles), scores_of, finish)
    arrivals.wait(*range(len(arrivals.copies)))


def attend(groups, heads, place, query, around, blocks, fresh_key, fresh_value):
    rows, width = query.shape[0], len(heads) * HD
    slots, count = len(OFFSETS), len(blocks)
    anywhere = pl.BlockSpec(memory_space=pl.ANY)
    return pl.pallas_call(
        functools.partial(attend_kernel, groups, 2 * count, heads[0]),
        in_specs=[pl.BlockSpec(memory_space=pltpu.SMEM)] + [anywhere] * (4 + 2 * count),
        out_specs=anywhere,
        out_shape=jax.ShapeDtypeStruct((slots, rows + STAT_ROWS, width), jnp.bfloat16),
        scratch_shapes=[
            pltpu.VMEM((slots * rows, width), jnp.bfloat16),
            pltpu.VMEM((count * rows, width), jnp.bfloat16),
            pltpu.VMEM((count * rows, width), jnp.bfloat16),
            pltpu.VMEM((rows, width), jnp.bfloat16),
            pltpu.VMEM((rows, width), jnp.bfloat16),
            pltpu.VMEM((slots, rows + STAT_ROWS, width), jnp.bfloat16),
            pltpu.SemaphoreType.DMA((2 * slots + 2 * count + 2,)),
        ],
        compiler_params=pltpu.CompilerParams(vmem_limit_bytes=BIG * 2**20),
        cost_estimate=attention_cost(slots * rows * count * rows * width),
        name="attend",
    )(
        place,
        query,
        around,
        *[array for block in blocks for array in block],
        fresh_key,
        fresh_value,
    )


def last_kernel(place_ref, keys_ref, values_ref, out_ref):
    for i in range(out_ref.shape[0]):
        out_ref[i] = place_ref[i]


def last_of(place, keys, values):
    smem, anywhere = pl.BlockSpec(memory_space=pltpu.SMEM), pl.BlockSpec(memory_space=pl.ANY)
    return pl.pallas_call(
        last_kernel,
        in_specs=[smem, anywhere, anywhere],
        out_specs=smem,
        out_shape=jax.ShapeDtypeStruct(place.shape, place.dtype),
        cost_estimate=pl.CostEstimate(flops=13 * 10**9, bytes_accessed=0, transcendentals=0),
        name="last_of",
    )(place, keys, values)


def repeat_kernel(a_ref, b_ref, out_ref):
    rows = a_ref.shape[0]
    out_ref[:rows, :] = a_ref[...]
    out_ref[rows:, :] = b_ref[...]


def repeat(a, b, times):
    rows, width = a.shape
    whole = pl.BlockSpec((rows, width), lambda i: (0, 0))
    return pl.pallas_call(
        repeat_kernel,
        grid=(times,),
        in_specs=[whole, whole],
        out_specs=pl.BlockSpec((None, 2 * rows, width), lambda i: (i, 0, 0)),
        out_shape=jax.ShapeDtypeStruct((times, 2 * rows, width), a.dtype),
        compiler_params=pltpu.CompilerParams(vmem_limit_bytes=BIG * 2**20),
        name="repeat",
    )(a, b)


def multiply_out(a_ref, w_ref, out_ref):
    for first in range(0, out_ref.shape[1], 2 * HD):
        columns = slice(first, first + 2 * HD)
        out_ref[:, columns] = jnp.dot(
            a_ref[...], w_ref[:, columns], preferred_element_type=jnp.float32
        ).astype(out_ref.dtype)


def combine_kernel(w_ref, *refs):
    *parts_refs, out_ref, first_ref, second_ref = refs
    group = parts_refs[0].shape[0]
    rows, width = out_ref.shape
    heads = width // HD
    where = [(ref, head_columns(i)) for ref in parts_refs for i in range(ref.shape[2] // HD)]
    shares = []
    for parts_ref, columns in where:
        lse = []
        for part in range(group):
            stat = parts_ref[part, rows:, columns].astype(jnp.float32)
            lines = stat[0:2] + stat[2:4] + stat[4:6]
            lse.append(jnp.concatenate([lines[:1], lines[1:2, : rows - HD]], axis=1))
        lse = jnp.concatenate(lse, axis=0)
        share = jnp.exp2(lse - jnp.max(lse, axis=0, keepdims=True))
        shares.append(share / jnp.sum(share, axis=0, keepdims=True))
    shares.append(jnp.zeros((HD - heads * group, rows), jnp.float32))
    by_row = jnp.transpose(jnp.concatenate(shares, axis=0))
    for head, (parts_ref, columns) in enumerate(where):
        total = jnp.zeros((rows, HD), jnp.float32)
        for part in range(group):
            at = head * group + part
            mixture = parts_ref[part, :rows, columns].astype(jnp.float32)
            total = total + by_row[:, at : at + 1] * mixture
        out_ref[:, head_columns(head)] = total.astype(jnp.bfloat16)
    for i, product_ref in enumerate((first_ref, second_ref)):
        multiply_out(out_ref, w_ref.at[i], product_ref)


def combine(weights, parts):
    rows = parts[0].shape[1] - STAT_ROWS
    _, width, columns = weights.shape
    return pl.pallas_call(
        combine_kernel,
        out_shape=[
            jax.ShapeDtypeStruct((rows, width), jnp.bfloat16),
            jax.ShapeDtypeStruct((rows, columns), jnp.bfloat16),
            jax.ShapeDtypeStruct((rows, columns), jnp.bfloat16),
        ],
        compiler_params=pltpu.CompilerParams(vmem_limit_bytes=SMALL * 2**20),
        name="combine",
    )(weights, *parts)


def select_kernel(block_ref, w_ref, out_ref):
    out_ref[...] = w_ref[...]


def select_columns(blocks, weight, columns):
    rows, count = weight.shape[0], blocks.shape[0]
    return pl.pallas_call(
        select_kernel,
        grid_spec=pltpu.PrefetchScalarGridSpec(
            num_scalar_prefetch=1,
            grid=(count,),
            in_specs=[pl.BlockSpec((rows, columns), lambda i, block: (0, block[i]))],
            out_specs=pl.BlockSpec((None, rows, columns), lambda i, block: (i, 0, 0)),
        ),
        out_shape=jax.ShapeDtypeStruct((count, rows, columns), weight.dtype),
        compiler_params=pltpu.CompilerParams(vmem_limit_bytes=SMALL * 2**20),
        name="select_columns",
    )(blocks, weight)


def project_kernel(block_ref, a_ref, w_ref, out_ref):
    multiply_out(a_ref, w_ref, out_ref)


def project(block, attended, out_weight, columns, dtype):
    rows, width = attended.shape
    steps = 2
    part = columns // steps
    return pl.pallas_call(
        project_kernel,
        grid_spec=pltpu.PrefetchScalarGridSpec(
            num_scalar_prefetch=1,
            grid=(steps,),
            in_specs=[
                pl.BlockSpec((rows, width), lambda i, block: (0, 0)),
                pl.BlockSpec((width, part), lambda i, block: (0, block[0] * steps + i)),
            ],
            out_specs=pl.BlockSpec((rows, part), lambda i, block: (0, i)),
        ),
        out_shape=jax.ShapeDtypeStruct((rows, columns), dtype),
        compiler_params=pltpu.CompilerParams(vmem_limit_bytes=SMALL * 2**20),
        name="project",
    )(block, attended, out_weight)


def move_z(array, step):
    return lax.ppermute(array, "z", [(z, (z + step) % NZ) for z in range(NZ)])


def shards(query, key_fresh, value_fresh, key_stale, value_stale, out_weight, residual, gate):
    columns = residual.shape[1]
    x_hi, core = lax.axis_index("x_hi"), lax.axis_index("core")

    swap = [(0, 1), (1, 0)]
    stacked = repeat(query, lax.ppermute(query, "x_lo", swap), NY)
    own = (key_stale, value_stale)
    up, down = [own], [own]
    for step in range(1, NZ // 2):
        up.append(tuple(move_z(array, 1) for array in up[-1]))
        down.append(tuple(move_z(array, -1) for array in down[-1]))
    stacked = lax.optimization_barrier((stacked, up[1][0], down[1][0]))[0]
    around = lax.all_to_all(stacked, "y", 0, 0)
    far = (move_z(up[-1][0], 1), move_z(down[-1][1], -1))
    place = jnp.stack([lax.axis_index("y"), lax.axis_index("x_lo")]).astype(jnp.int32)
    place = last_of(place, *far)
    heads = query.shape[1] // HD
    partials = attend(
        ((2, 3), (4, 5), (6, 7), (1,), (0,)),
        range(heads),
        place,
        query,
        around,
        up + down[1:] + [far],
        key_fresh,
        value_fresh,
    )
    returned = [lax.all_to_all(partials, ("y", "x_lo"), 0, 0)]

    def block(x_half, core_half):
        return (x_half * 2 + core_half).astype(jnp.int32).reshape(1)

    both = jnp.concatenate([block(1 - x_hi, 1 - core), block(x_hi, 1 - core)])
    both, own_block, _ = lax.optimization_barrier((both, block(1 - x_hi, core), partials))
    own_weight = select_columns(own_block, out_weight, columns)[0]
    attended, for_core, for_core_late = combine(
        select_columns(both, out_weight, columns), returned
    )
    from_core = lax.ppermute(for_core, "core", swap).astype(jnp.float32)
    chip_sum = project(jnp.zeros_like(own_block), attended, own_weight, columns, jnp.float32)
    chip_sum = (chip_sum + from_core).astype(jnp.bfloat16)
    from_x = lax.ppermute(chip_sum, "x_hi", swap)
    attended, for_core_late, _ = lax.optimization_barrier((attended, for_core_late, chip_sum))
    from_core = lax.ppermute(for_core_late, "core", swap)
    total = project(block(x_hi, core), attended, out_weight, columns, jnp.float32)
    gate_row = gate.astype(jnp.float32)[None, :]
    total = total + from_core.astype(jnp.float32)
    ready = lax.optimization_barrier(residual.astype(jnp.float32) + gate_row * total)
    return (ready + gate_row * from_x.astype(jnp.float32)).astype(jnp.bfloat16)


def solution(mesh):
    axes = ("y", "x_lo", "z", "x_hi", "core")
    fine = Mesh(mesh.devices.reshape(NY, NX, NZ, 2, 2), axes)
    rows, cols = ("y", "x_lo", "z"), ("x_hi", "core")
    return jax.shard_map(
        shards,
        mesh=fine,
        in_specs=(
            P(rows, cols),
            P(rows, cols),
            P(rows, cols),
            P(rows, cols),
            P(rows, cols),
            P(cols, None),
            P(rows, cols),
            P(cols),
        ),
        out_specs=P(rows, cols),
        check_vma=False,
    )
```
